32 devices in a mesh: gx: 4 (over y, core), gy: 8 (over z, x).
Axes of the slice: x: 2, y: 2, z: 4, core: 2. Of those that a mesh axis runs over, the one named last changes fastest.
Arguments:
- positions: float32 [4, 8, 3, 8192], P('gx', 'gy'), may hold values from 0 to 3
- velocities: float32 [4, 8, 3, 8192], P('gx', 'gy'), may hold values from -5 to 5
- spins: float32 [4, 8, 3, 8192], P('gx', 'gy'), may hold values from -5 to 5
- radii: float32 [4, 8, 8192], P('gx', 'gy'), may hold values from 0.4 to 0.6
- counts: int32 [4, 8], P('gx', 'gy'), may hold values from 1024 to 8192
- exports: int32 [4, 8, 8, 32], P('gx', 'gy'), may hold values from 0 to 63
- partners: int32 [4, 8, 128], P('gx', 'gy'), may hold values from 0 to 319
- masks: int32 [4, 8, 128, 16, 128], P('gx', 'gy'), may hold values from 0 to 255
Outputs:
- new_positions: float32 [4, 8, 3, 8192], P('gx', 'gy')
- new_velocities: float32 [4, 8, 3, 8192], P('gx', 'gy')
- new_spins: float32 [4, 8, 3, 8192], P('gx', 'gy')
The draws below stay inside these ranges and needn't reach their ends.
Inputs may be any that keep to these rules, and one draw needn't show every extreme that they name: The first counts spheres of a column are live; the others take no part. `exports`: indices of owned tiles; a tile may appear more than once. `partners`: slots below 64 are owned tiles, the others ghost tiles. `masks`: each word holds 8 bits.
All inputs are finite; a program needn't handle non-finite values.
Results may differ from the reference program's by a relative error of at most 0.0003.
Values sent between devices are 32-bit elements; how exact they have to be, the bound alone decides.
A program may use at most 64 MiB of HBM per device.

```python
import math
import jax
import jax.numpy as jnp
import numpy as np
from jax import lax

TILE = 128
TILES = 64
EXPORT = 32
PARTNERS = 2
STEPS = 2
SPHERES = 8192
PAIRS = 128
SLOTS = 320
N_GX = 4
N_GY = 8


def touch_ends(entries, rng, low, high):
    index_at = [jax.random.randint(jax.random.fold_in(rng, axis), (), 0, length) for axis, length in enumerate(entries.shape)]
    widest = entries.shape.index(max(entries.shape))
    next_to = index_at[:widest] + [(index_at[widest] + 1) % entries.shape[widest]] + index_at[widest + 1:]
    return entries.at[tuple(index_at)].set(low).at[tuple(next_to)].set(high)


def levels(own_key, dims, shards, least, largest):
    factor_of, own = 1.0, jax.random.fold_in(own_key, 6)
    for axis_at, blocks in shards:
        heights = jnp.exp(jax.random.uniform(jax.random.fold_in(own, axis_at), (blocks,), jnp.float32, least / len(shards), largest / len(shards)))
        factor_of = factor_of * jnp.repeat(heights, dims[axis_at] // blocks).reshape([-1 if axis == axis_at else 1 for axis in range(len(dims))])
    return factor_of


def centred(own_key, extent, deviation, bound, cuts=(), held_as=jnp.bfloat16):
    level = levels(own_key, extent, cuts, -0.22, 0.18) if cuts else 1.0
    drawn = jax.random.normal(own_key, extent, jnp.float32) * deviation * level
    return jnp.minimum(jnp.maximum(drawn, -bound), bound).astype(held_as)


def setup_inputs(seed: int = 0) -> dict:
    streams_of = jax.random.split(jax.random.key(seed), 9)
    return {
        "positions": jnp.clip(3.0 * jax.random.uniform(streams_of[0], (N_GX, N_GY, 3, SPHERES), jnp.float32) ** levels(streams_of[0], (N_GX, N_GY, 3, SPHERES), ((0, 4), (1, 8)), -0.2, 0.2), 0.0, 3.0),
        "velocities": centred(streams_of[1], (N_GX, N_GY, 3, SPHERES), 1.0, 5.0, ((0, 4), (1, 8)), jnp.float32),
        "spins": centred(streams_of[2], (N_GX, N_GY, 3, SPHERES), 1.0, 5.0, ((0, 4), (1, 8)), jnp.float32),
        "radii": jnp.clip(jnp.exp(math.log(0.6) - 0.40546513 * jax.random.uniform(streams_of[3], (N_GX, N_GY, SPHERES), jnp.float32) ** levels(streams_of[3], (N_GX, N_GY, SPHERES), ((0, 4), (1, 8)), -0.2, 0.2)), 0.4, 0.6),
        "counts": touch_ends(jax.random.randint(streams_of[4], (N_GX, N_GY), SPHERES // 8, SPHERES + 1), jax.random.fold_in(streams_of[4], 1), SPHERES // 8, SPHERES).astype(jnp.int32),
        "exports": touch_ends(jax.random.randint(streams_of[5], (N_GX, N_GY, 8, EXPORT), 0, TILES), jax.random.fold_in(streams_of[5], 1), 0, TILES - 1).astype(jnp.int32),
        "partners": touch_ends(jax.random.randint(streams_of[6], (N_GX, N_GY, PAIRS), 0, SLOTS), jax.random.fold_in(streams_of[6], 1), 0, SLOTS - 1).astype(jnp.int32),
        "masks": touch_ends(jax.random.randint(streams_of[7], (N_GX, N_GY, PAIRS, 16, TILE), 0, 256), jax.random.fold_in(streams_of[7], 1), 0, 255).astype(jnp.int32),
    }


stiffness = 1.0
damping_normal = 0.5
damping_tangent = 0.3
softening = 0.05
time_step = 0.25
column_width = 3.0
gravity = 1.0
mass_scale = 8.0
offsets = ((1, 0), (-1, 0), (0, 1), (0, -1), (1, 1), (1, -1), (-1, 1), (-1, -1))

def unpack_bits(words):
    shifts = jnp.arange(8, dtype=jnp.int32)
    bits = jnp.bitwise_and(jnp.right_shift(words[:, :, None, :], shifts[None, None, :, None]), 1)
    bits = bits.reshape(words.shape[0], words.shape[1] * 8, words.shape[2])
    return jnp.swapaxes(bits, 1, 2).astype(jnp.float32)

def cross(left, right):
    return (left[1] * right[2] - left[2] * right[1], left[2] * right[0] - left[0] * right[2], left[0] * right[1] - left[1] * right[0])

def block_forces(tiles, partner, words, first):
    number = partner.shape[0]
    slots = tiles.shape[1]
    owner = ((first + jnp.arange(number, dtype=jnp.int32)) // PARTNERS).astype(jnp.int32)
    left = jnp.take(tiles, owner, axis=1)[:, :, :, None]
    right = jnp.take(tiles, partner, axis=1)[:, :, None, :]
    weight = unpack_bits(words) * left[10] * right[10]
    separation = [right[k] - left[k] for k in range(3)]
    dist = jnp.sqrt(separation[0] * separation[0] + separation[1] * separation[1] + separation[2] * separation[2] + softening * softening)
    normal = [c / dist for c in separation]
    rad_i = left[9]
    rad_j = right[9]
    intersection = jnp.maximum(rad_i + rad_j - dist, 0.0)
    root = jnp.sqrt(rad_i * rad_j / (rad_i + rad_j) * intersection)
    spin_sum = [rad_i * left[6 + k] + rad_j * right[6 + k] for k in range(3)]
    turning = cross(spin_sum, normal)
    slip = [right[3 + k] - left[3 + k] - turning[k] for k in range(3)]
    speed_n = slip[0] * normal[0] + slip[1] * normal[1] + slip[2] * normal[2]
    push = weight * root * (stiffness * intersection - damping_normal * speed_n)
    drag = weight * root * damping_tangent
    force_j = [push * normal[k] - drag * (slip[k] - speed_n * normal[k]) for k in range(3)]
    twist = cross(normal, force_j)
    own_terms = jnp.stack([-lax.optimization_barrier(jnp.sum(f, axis=2)) for f in force_j] + [-lax.optimization_barrier(jnp.sum(rad_i * t, axis=2)) for t in twist], axis=1)
    other_terms = jnp.stack([lax.optimization_barrier(jnp.sum(f, axis=1)) for f in force_j] + [-lax.optimization_barrier(jnp.sum(rad_j * t, axis=1)) for t in twist], axis=1)
    places = jnp.arange(slots, dtype=jnp.int32)
    own_hot = (owner[:, None] == places[None, :]).astype(jnp.float32)
    other_hot = (partner[:, None] == places[None, :]).astype(jnp.float32)
    total = jnp.einsum('pt,pcs->cts', own_hot, own_terms, precision=lax.Precision.HIGHEST)
    return total + jnp.einsum('pt,pcs->cts', other_hot, other_terms, precision=lax.Precision.HIGHEST)

def contact_forces(tiles, partners, words, blocks):
    size = 4 * PARTNERS

    def one_block(index, total):
        first = (index * size).astype(jnp.int32)
        part = lax.dynamic_slice_in_dim(partners, first, size, 0)
        word = lax.dynamic_slice_in_dim(words, first, size, 0)
        return total + block_forces(tiles, part, word, first)
    start = jnp.zeros((6, tiles.shape[1], tiles.shape[2]), jnp.float32)
    return lax.fori_loop(0, blocks, one_block, start)

def advance(position, velocity, spin, radius, live, force):
    mass = mass_scale * radius * radius * radius
    inertia = 0.4 * mass * radius * radius
    lift = jnp.array([0.0, 0.0, -gravity], jnp.float32)[:, None, None]
    velocity = velocity + time_step * live * (force[..., 0:3, :, :] / mass + lift)
    spin = spin + time_step * live * force[..., 3:6, :, :] / inertia
    position = position + time_step * live * velocity
    return (position, velocity, spin)

def reference(positions, velocities, spins, radii, counts, exports, partners, masks):
    cols_x = positions.shape[0]
    cols_y = positions.shape[1]
    index = jnp.arange(TILES * TILE, dtype=jnp.int32)
    live = (index[None, None, :] < counts[:, :, None]).astype(jnp.float32)
    live = live.reshape(cols_x, cols_y, 1, TILES, TILE)
    radius = radii.reshape(cols_x, cols_y, 1, TILES, TILE)
    position = positions.reshape(cols_x, cols_y, 3, TILES, TILE)
    velocity = velocities.reshape(cols_x, cols_y, 3, TILES, TILE)
    spin = spins.reshape(cols_x, cols_y, 3, TILES, TILE)
    blocks = PAIRS // (4 * PARTNERS)
    places = jnp.arange(TILES, dtype=jnp.int32)

    def pick(state, chosen):
        taken = jnp.take(state, chosen.reshape(-1), axis=1)
        return taken.reshape(state.shape[0], 8, chosen.shape[1], TILE)
    for step in range(STEPS):
        state = jnp.concatenate([position, velocity, spin, radius, live], axis=2)
        sent = jax.vmap(jax.vmap(pick))(state, exports)
        pieces = [state]
        for which in range(8):
            step_x, step_y = offsets[which]
            block = jnp.roll(sent[:, :, :, which], (step_x, step_y), axis=(0, 1))
            moved = np.zeros((11, 1, 1), np.float32)
            moved[0] = -step_x * column_width
            moved[1] = -step_y * column_width
            pieces.append(block + jnp.asarray(moved))
        tiles = jnp.concatenate(pieces, axis=3)
        flat = tiles.reshape(cols_x * cols_y, 11, tiles.shape[3], TILE)
        flat_pairs = partners.reshape(cols_x * cols_y, PAIRS)
        flat_masks = masks.reshape(cols_x * cols_y, PAIRS, 16, TILE)
        force = lax.map(lambda item: contact_forces(item[0], item[1], item[2], blocks), (flat, flat_pairs, flat_masks))
        force = force.reshape(cols_x, cols_y, 6, tiles.shape[3], TILE)
        total = force[:, :, :, :TILES]
        for which in range(8):
            step_x, step_y = offsets[which]
            slot = force[:, :, :, TILES + which * EXPORT:TILES + (which + 1) * EXPORT]
            back = jnp.roll(slot, (-step_x, -step_y), axis=(0, 1))
            chooser = (exports[:, :, which, :, None] == places).astype(jnp.float32)
            total = total + jnp.einsum('xyet,xycea->xycta', chooser, back, precision=lax.Precision.HIGHEST)
        position, velocity, spin = advance(position, velocity, spin, radius, live, total)
    shape = (cols_x, cols_y, 3, TILES * TILE)
    return (position.reshape(shape), velocity.reshape(shape), spin.reshape(shape))
```

```python
import functools

import jax
import jax.numpy as jnp
from jax import lax
from jax.experimental import pallas as pl
from jax.experimental.pallas import tpu as pltpu
from jax.sharding import PartitionSpec as P

TILE = 128
PARTNERS = 2
STEPS = 2
FIELDS = 9

softening = 0.05
time_step = 0.25
column_width = 3.0
gravity = 1.0
mass_scale = 8.0
offsets = ((1, 0), (-1, 0), (0, 1), (0, -1), (1, 1), (1, -1), (-1, 1), (-1, -1))
order = (2, 3, 4, 5, 6, 7, 0, 1)

MESH = pl.DeviceIdType.MESH
VMEM = pl.BlockSpec(memory_space=pltpu.VMEM)
SMEM = pl.BlockSpec(memory_space=pltpu.SMEM)
LIMIT = 40 * 1024 * 1024


def neighbour(sizes, which, sign):
    a, b = offsets[which]
    nx, ny = sizes
    x = lax.rem(lax.axis_index("gx") + sign * a + nx, nx)
    y = lax.rem(lax.axis_index("gy") + sign * b + ny, ny)
    return (x, y)


def greet(sizes):
    barrier = pltpu.get_barrier_semaphore()
    for which in range(8):
        pl.semaphore_signal(
            barrier, inc=1, device_id=neighbour(sizes, which, 1), device_id_type=MESH
        )
    pl.semaphore_wait(barrier, 8)


def gather_tiles(chosen, state, sent, which, per_side):
    a, b = offsets[which]
    moved = (-a * column_width, -b * column_width)

    def one(e, carry):
        tile = chosen[which * per_side + e]
        for f in range(FIELDS):
            row = state[f, pl.ds(tile, 1), :]
            if f < 2 and moved[f] != 0.0:
                row = row + moved[f]
            sent[f, pl.ds(which * per_side + e, 1), :] = row
        return carry

    lax.fori_loop(0, per_side, one, 0, unroll=4)


def send_records(sizes, chosen, state, sent, slots, send_sem, recv_sem, per_side, tiles_own):
    copies = []
    for which in order:
        gather_tiles(chosen, state, sent, which, per_side)
        copy = pltpu.make_async_remote_copy(
            src_ref=sent.at[:, pl.ds(which * per_side, per_side), :],
            dst_ref=slots.at[:, pl.ds(tiles_own + which * per_side, per_side), :],
            send_sem=send_sem.at[which],
            recv_sem=recv_sem.at[which],
            device_id=neighbour(sizes, which, 1),
            device_id_type=MESH,
        )
        copy.start()
        copies.append(copy)
    slots[:, 0:tiles_own, :] = state[...]
    return copies


def first_kernel(
    sizes, per_side, tiles_own, chosen, state, radius, reach,
    slots, radii, reaches, sent, sent_radius, send_sem, recv_sem, rad_send, rad_recv,
    reach_send, reach_recv,
):
    greet(sizes)
    copies = send_records(
        sizes, chosen, state, sent, slots, send_sem, recv_sem, per_side, tiles_own
    )
    for which in order:
        def one(e, carry):
            tile = chosen[which * per_side + e]
            sent_radius[pl.ds(which * per_side + e, 1), :] = radius[pl.ds(tile, 1), :]
            return carry

        lax.fori_loop(0, per_side, one, 0, unroll=4)
        to = neighbour(sizes, which, 1)
        copy = pltpu.make_async_remote_copy(
            src_ref=sent_radius.at[pl.ds(which * per_side, per_side), :],
            dst_ref=radii.at[pl.ds(tiles_own + which * per_side, per_side), :],
            send_sem=rad_send.at[which],
            recv_sem=rad_recv.at[which],
            device_id=to,
            device_id_type=MESH,
        )
        copy.start()
        copies.append(copy)
        copy = pltpu.make_async_remote_copy(
            src_ref=reach.at[which],
            dst_ref=reaches.at[which],
            send_sem=reach_send.at[which],
            recv_sem=reach_recv.at[which],
            device_id=to,
            device_id_type=MESH,
        )
        copy.start()
        copies.append(copy)
    radii[0:tiles_own, :] = radius[...]
    for copy in copies:
        copy.wait()


def start_returns(sizes, force, back, send_sem, recv_sem, per_side, tiles_own):
    copies = []
    for which in order:
        copy = pltpu.make_async_remote_copy(
            src_ref=force.at[:, pl.ds(tiles_own + which * per_side, per_side), :],
            dst_ref=back.at[:, pl.ds(which * per_side, per_side), :],
            send_sem=send_sem.at[which],
            recv_sem=recv_sem.at[which],
            device_id=neighbour(sizes, which, -1),
            device_id_type=MESH,
        )
        copy.start()
        copies.append(copy)
    return copies


def advance(chooser, state, radius, live, force, back, moved, tiles_own):
    rad = radius[...]
    alive = time_step * live[...]
    mass = mass_scale * rad * rad * rad
    inertia = 0.4 * mass * rad * rad
    hot = chooser[...]
    total = []
    for f in range(6):
        values = back[f]
        high = values.astype(jnp.bfloat16)
        rest = values - high.astype(jnp.float32)
        middle = rest.astype(jnp.bfloat16)
        low = (rest - middle.astype(jnp.float32)).astype(jnp.bfloat16)
        summed = force[f, 0:tiles_own, :]
        for part in (low, middle, high):
            summed = summed + jnp.dot(hot, part, preferred_element_type=jnp.float32)
        total.append(summed)
    for k in range(3):
        pull = total[k] / mass
        if k == 2:
            pull = pull - gravity
        velocity = state[3 + k] + alive * pull
        moved[3 + k] = velocity
        moved[6 + k] = state[6 + k] + alive * total[3 + k] / inertia
        moved[k] = state[k] + alive * velocity


def middle_kernel(
    sizes, per_side, tiles_own, chosen, chooser, state, radius, live, force,
    moved, slots, sent, back, back_send, back_recv, send_sem, recv_sem,
):
    greet(sizes)
    for copy in start_returns(sizes, force, back, back_send, back_recv, per_side, tiles_own):
        copy.wait()
    advance(chooser, state, radius, live, force, back, moved, tiles_own)
    copies = send_records(
        sizes, chosen, moved, sent, slots, send_sem, recv_sem, per_side, tiles_own
    )
    for copy in copies:
        copy.wait()


def last_kernel(
    sizes, per_side, tiles_own, chooser, state, radius, live, force,
    moved, back, back_send, back_recv,
):
    greet(sizes)
    for copy in start_returns(sizes, force, back, back_send, back_recv, per_side, tiles_own):
        copy.wait()
    advance(chooser, state, radius, live, force, back, moved, tiles_own)


def cross(left, right):
    return (
        left[1] * right[2] - left[2] * right[1],
        left[2] * right[0] - left[0] * right[2],
        left[0] * right[1] - left[1] * right[0],
    )


def pair_kernel(tiles_own, partner, reach, slots, radii, masks, force, record):
    force[...] = jnp.zeros_like(force)
    sub = lax.broadcasted_iota(jnp.int32, (8, TILE), 0)
    lane = lax.broadcasted_iota(jnp.int32, (8, TILE), 1)
    bit = lax.shift_left(jnp.ones_like(sub), sub)
    word_sub = lax.broadcasted_iota(jnp.int32, (16, TILE), 0)
    word_lane = lax.broadcasted_iota(jnp.int32, (16, TILE), 1)
    record[...] = jnp.zeros_like(record)

    def one_pair(p, t, slot, reach_i, reach_j):
        rad_i = radii[pl.ds(t, 1), :]
        own = [slots[f, pl.ds(t, 1), :] for f in range(FIELDS)]
        own = own[:6] + [rad_i * w for w in own[6:]]
        own = [jnp.broadcast_to(f, (8, TILE)) for f in own + [rad_i]]
        rad_j_row = radii[pl.ds(slot, 1), :]
        for f in range(FIELDS):
            row = slots[f, pl.ds(slot, 1), :]
            record[f : f + 1, :] = row if f < 6 else rad_j_row * row
        record[FIELDS : FIELDS + 1, :] = rad_j_row
        other = record[...].T
        valid = lax.shift_left(
            jnp.ones_like(word_sub), jnp.clip(reach_j - 8 * word_sub, 0, 8)
        ) - 1
        words = jnp.where(word_lane < reach_i, masks[p] & valid, 0)
        sums = [jnp.zeros((8, TILE), jnp.float32) for _ in range(6)]
        columns = []
        for c in range(TILE // 8):
            right = [
                jnp.broadcast_to(other[8 * c : 8 * c + 8, f : f + 1], (8, TILE))
                for f in range(FIELDS + 1)
            ]
            on = (jnp.broadcast_to(words[c : c + 1, :], (8, TILE)) & bit) != 0
            sep = [right[k] - own[k] for k in range(3)]
            square = (
                sep[0] * sep[0] + sep[1] * sep[1] + (sep[2] * sep[2] + softening * softening)
            )
            inverse = lax.rsqrt(square)
            normal = [s * inverse for s in sep]
            reach_sum = own[9] + right[9]
            inter = jnp.maximum(reach_sum - square * inverse, 0.0)
            inner = own[9] * right[9] * inter
            root = inner * lax.rsqrt(jnp.maximum(inner * reach_sum, 1e-36))
            scale = jnp.where(on, root, 0.0)
            spin_sum = [own[6 + k] + right[6 + k] for k in range(3)]
            turning = cross(spin_sum, normal)
            slip = [right[3 + k] - own[3 + k] - turning[k] for k in range(3)]
            speed = slip[0] * normal[0] + slip[1] * normal[1] + slip[2] * normal[2]
            push = scale * (inter - 0.2 * speed)
            drag = 0.3 * scale
            pushed = [push * normal[k] - drag * slip[k] for k in range(3)]
            terms = pushed + list(cross(normal, pushed))
            column = jnp.zeros((8, TILE), jnp.float32)
            for k in range(6):
                sums[k] = sums[k] + terms[k]
                column = jnp.where(lane == k, jnp.sum(terms[k], axis=1, keepdims=True), column)
            columns.append(column)
        others = jnp.concatenate(columns, axis=0).T
        for k in range(6):
            mine = jnp.sum(sums[k], axis=0, keepdims=True)
            if k >= 3:
                mine = rad_i * mine
            force[k, pl.ds(t, 1), :] = force[k, pl.ds(t, 1), :] - mine
        for k in range(6):
            theirs = others[k : k + 1, :]
            if k >= 3:
                theirs = -rad_j_row * theirs
            force[k, pl.ds(slot, 1), :] = force[k, pl.ds(slot, 1), :] + theirs

    def one(p, carry):
        t = p // PARTNERS
        slot = partner[p]
        reach_i = reach[t]
        reach_j = reach[slot]

        @pl.when(jnp.logical_and(reach_i > 0, reach_j > 0))
        def _():
            one_pair(p, t, slot, reach_i, reach_j)

        return carry

    lax.fori_loop(0, partner.shape[0], one, 0)


def local(sizes, positions, velocities, spins, radii, counts, exports, partners, masks):
    tiles_own = radii.shape[-1] // TILE
    per_side = exports.shape[-1]
    ghosts = 8 * per_side
    slots_all = tiles_own + ghosts
    count = counts[0, 0]
    chosen = exports[0, 0].reshape(-1)
    partner = partners[0, 0]
    words = masks[0, 0]
    starts = TILE * jnp.arange(tiles_own, dtype=jnp.int32)
    own_reach = jnp.clip(count - starts, 0, TILE)
    sent_reach = jnp.clip(count - TILE * exports[0, 0], 0, TILE)
    sent_reach = jnp.pad(sent_reach[:, None, :], ((0, 0), (0, 7), (0, TILE - per_side)))
    index = jnp.arange(tiles_own * TILE, dtype=jnp.int32)
    live = (index < count).astype(jnp.float32).reshape(tiles_own, TILE)
    radius = radii[0, 0].reshape(tiles_own, TILE)
    state = jnp.concatenate([positions[0, 0], velocities[0, 0], spins[0, 0]], axis=0)
    state = state.reshape(FIELDS, tiles_own, TILE)
    places = jnp.arange(tiles_own, dtype=jnp.int32)
    chooser = (places[:, None] == chosen[None, :]).astype(jnp.bfloat16)

    f32 = jnp.float32
    slots_shape = jax.ShapeDtypeStruct((FIELDS, slots_all, TILE), f32)
    state_shape = jax.ShapeDtypeStruct((FIELDS, tiles_own, TILE), f32)
    sent = pltpu.VMEM((FIELDS, ghosts, TILE), f32)
    back = pltpu.VMEM((6, ghosts, TILE), f32)
    dma = pltpu.SemaphoreType.DMA((8,))

    def params(number):
        return pltpu.CompilerParams(
            collective_id=number, has_side_effects=True, vmem_limit_bytes=LIMIT
        )

    slots, radii_all, reaches = pl.pallas_call(
        functools.partial(first_kernel, sizes, per_side, tiles_own),
        out_shape=(
            slots_shape,
            jax.ShapeDtypeStruct((slots_all, TILE), f32),
            jax.ShapeDtypeStruct((8, 8, TILE), jnp.int32),
        ),
        in_specs=[SMEM, VMEM, VMEM, VMEM],
        out_specs=(VMEM, VMEM, VMEM),
        scratch_shapes=[sent, pltpu.VMEM((ghosts, TILE), f32)] + [dma] * 6,
        compiler_params=params(0),
        name="send_first",
    )(chosen, state, radius, sent_reach)
    reach = jnp.concatenate([own_reach, reaches[:, 0, :per_side].reshape(-1)])

    def pair_forces(slots):
        return pl.pallas_call(
            functools.partial(pair_kernel, tiles_own),
            out_shape=jax.ShapeDtypeStruct((6, slots_all, TILE), f32),
            in_specs=[SMEM, SMEM, VMEM, VMEM, VMEM],
            out_specs=VMEM,
            scratch_shapes=[pltpu.VMEM((16, TILE), f32)],
            compiler_params=pltpu.CompilerParams(vmem_limit_bytes=LIMIT),
            name="pair_forces",
        )(partner, reach, slots, radii_all, words)

    for step in range(STEPS):
        force = pair_forces(slots)
        if step < STEPS - 1:
            state, slots = pl.pallas_call(
                functools.partial(middle_kernel, sizes, per_side, tiles_own),
                out_shape=(state_shape, slots_shape),
                in_specs=[SMEM] + [VMEM] * 5,
                out_specs=(VMEM, VMEM),
                scratch_shapes=[sent, back] + [dma] * 4,
                compiler_params=params(1 + step),
                name="return_advance_send",
            )(chosen, chooser, state, radius, live, force)
        else:
            state = pl.pallas_call(
                functools.partial(last_kernel, sizes, per_side, tiles_own),
                out_shape=state_shape,
                in_specs=[VMEM] * 5,
                out_specs=VMEM,
                scratch_shapes=[back] + [dma] * 2,
                compiler_params=params(1 + step),
                name="return_advance",
            )(chooser, state, radius, live, force)
    shape = (1, 1, 3, tiles_own * TILE)
    return tuple(state[3 * k : 3 * k + 3].reshape(shape) for k in range(3))


def solution(mesh):
    sizes = (mesh.shape["gx"], mesh.shape["gy"])
    return jax.shard_map(
        functools.partial(local, sizes),
        mesh=mesh,
        in_specs=(
            P("gx", "gy", None, None),
            P("gx", "gy", None, None),
            P("gx", "gy", None, None),
            P("gx", "gy", None),
            P("gx", "gy"),
            P("gx", "gy", None, None),
            P("gx", "gy", None),
            P("gx", "gy", None, None, None),
        ),
        out_specs=(P("gx", "gy", None, None), P("gx", "gy", None, None), P("gx", "gy", None, None)),
        check_vma=False,
    )
```

```python
import functools

import jax
import jax.numpy as jnp
from jax import lax
from jax.experimental import pallas as pl
from jax.experimental.pallas import tpu as pltpu
from jax.sharding import PartitionSpec as P

TILE = 128
PARTNERS = 2
STEPS = 2
FIELDS = 9

softening = 0.05
time_step = 0.25
column_width = 3.0
gravity = 1.0
mass_scale = 8.0
offsets = ((1, 0), (-1, 0), (0, 1), (0, -1), (1, 1), (1, -1), (-1, 1), (-1, -1))
order = (2, 3, 4, 5, 6, 7, 0, 1)

MESH = pl.DeviceIdType.MESH
VMEM = pl.BlockSpec(memory_space=pltpu.VMEM)
SMEM = pl.BlockSpec(memory_space=pltpu.SMEM)
LIMIT = 40 * 1024 * 1024


def neighbour(sizes, which, sign):
    a, b = offsets[which]
    nx, ny = sizes
    x = lax.rem(lax.axis_index("gx") + sign * a + nx, nx)
    y = lax.rem(lax.axis_index("gy") + sign * b + ny, ny)
    return (x, y)


def greet(sizes):
    barrier = pltpu.get_barrier_semaphore()
    for which in range(8):
        pl.semaphore_signal(
            barrier, inc=1, device_id=neighbour(sizes, which, 1), device_id_type=MESH
        )
    pl.semaphore_wait(barrier, 8)


def gather_tiles(chosen, state, sent, which, per_side):
    a, b = offsets[which]
    moved = (-a * column_width, -b * column_width)

    def one(e, carry):
        tile = chosen[which * per_side + e]
        for f in range(FIELDS):
            row = state[f, pl.ds(tile, 1), :]
            if f < 2 and moved[f] != 0.0:
                row = row + moved[f]
            sent[f, pl.ds(which * per_side + e, 1), :] = row
        return carry

    lax.fori_loop(0, per_side, one, 0, unroll=4)


def send_records(sizes, chosen, state, sent, slots, send_sem, recv_sem, per_side, tiles_own):
    copies = []
    for which in order:
        gather_tiles(chosen, state, sent, which, per_side)
        copy = pltpu.make_async_remote_copy(
            src_ref=sent.at[:, pl.ds(which * per_side, per_side), :],
            dst_ref=slots.at[:, pl.ds(tiles_own + which * per_side, per_side), :],
            send_sem=send_sem.at[which],
            recv_sem=recv_sem.at[which],
            device_id=neighbour(sizes, which, 1),
            device_id_type=MESH,
        )
        copy.start()
        copies.append(copy)
    slots[:, 0:tiles_own, :] = state[...]
    return copies


def first_kernel(
    sizes, per_side, tiles_own, chosen, state, radius, reach,
    slots, radii, reaches, sent, sent_radius, send_sem, recv_sem, rad_send, rad_recv,
    reach_send, reach_recv,
):
    greet(sizes)
    copies = send_records(
        sizes, chosen, state, sent, slots, send_sem, recv_sem, per_side, tiles_own
    )
    for which in order:
        def one(e, carry):
            tile = chosen[which * per_side + e]
            sent_radius[pl.ds(which * per_side + e, 1), :] = radius[pl.ds(tile, 1), :]
            return carry

        lax.fori_loop(0, per_side, one, 0, unroll=4)
        to = neighbour(sizes, which, 1)
        copy = pltpu.make_async_remote_copy(
            src_ref=sent_radius.at[pl.ds(which * per_side, per_side), :],
            dst_ref=radii.at[pl.ds(tiles_own + which * per_side, per_side), :],
            send_sem=rad_send.at[which],
            recv_sem=rad_recv.at[which],
            device_id=to,
            device_id_type=MESH,
        )
        copy.start()
        copies.append(copy)
        copy = pltpu.make_async_remote_copy(
            src_ref=reach.at[which],
            dst_ref=reaches.at[which],
            send_sem=reach_send.at[which],
            recv_sem=reach_recv.at[which],
            device_id=to,
            device_id_type=MESH,
        )
        copy.start()
        copies.append(copy)
    radii[0:tiles_own, :] = radius[...]
    for copy in copies:
        copy.wait()


def start_returns(sizes, force, back, send_sem, recv_sem, per_side, tiles_own):
    copies = []
    for which in order:
        copy = pltpu.make_async_remote_copy(
            src_ref=force.at[:, pl.ds(tiles_own + which * per_side, per_side), :],
            dst_ref=back.at[:, pl.ds(which * per_side, per_side), :],
            send_sem=send_sem.at[which],
            recv_sem=recv_sem.at[which],
            device_id=neighbour(sizes, which, -1),
            device_id_type=MESH,
        )
        copy.start()
        copies.append(copy)
    return copies


def advance(chooser, state, radius, live, force, back, moved, tiles_own):
    rad = radius[...]
    alive = time_step * live[...]
    mass = mass_scale * rad * rad * rad
    inertia = 0.4 * mass * rad * rad
    hot = chooser[...]
    total = []
    for f in range(6):
        values = back[f]
        high = values.astype(jnp.bfloat16)
        rest = values - high.astype(jnp.float32)
        middle = rest.astype(jnp.bfloat16)
        low = (rest - middle.astype(jnp.float32)).astype(jnp.bfloat16)
        summed = force[f, 0:tiles_own, :]
        for part in (low, middle, high):
            summed = summed + jnp.dot(hot, part, preferred_element_type=jnp.float32)
        total.append(summed)
    for k in range(3):
        pull = total[k] / mass
        if k == 2:
            pull = pull - gravity
        velocity = state[3 + k] + alive * pull
        moved[3 + k] = velocity
        moved[6 + k] = state[6 + k] + alive * total[3 + k] / inertia
        moved[k] = state[k] + alive * velocity


def middle_kernel(
    sizes, per_side, tiles_own, chosen, chooser, state, radius, live, force,
    moved, slots, sent, back, back_send, back_recv, send_sem, recv_sem,
):
    greet(sizes)
    for copy in start_returns(sizes, force, back, back_send, back_recv, per_side, tiles_own):
        copy.wait()
    advance(chooser, state, radius, live, force, back, moved, tiles_own)
    copies = send_records(
        sizes, chosen, moved, sent, slots, send_sem, recv_sem, per_side, tiles_own
    )
    for copy in copies:
        copy.wait()


def last_kernel(
    sizes, per_side, tiles_own, chooser, state, radius, live, force,
    moved, back, back_send, back_recv,
):
    greet(sizes)
    for copy in start_returns(sizes, force, back, back_send, back_recv, per_side, tiles_own):
        copy.wait()
    advance(chooser, state, radius, live, force, back, moved, tiles_own)


def cross(left, right):
    return (
        left[1] * right[2] - left[2] * right[1],
        left[2] * right[0] - left[0] * right[2],
        left[0] * right[1] - left[1] * right[0],
    )


def split(values, parts):
    pieces = []
    for _ in range(parts - 1):
        piece = values.astype(jnp.bfloat16)
        pieces.append(piece)
        values = values - piece.astype(jnp.float32)
    return pieces + [values.astype(jnp.bfloat16)]


def pair_kernel(
    tiles_own, partner, reach, slots, radii, masks, force, record, spread, fields, terms_hold, pick
):
    bf16, f32 = jnp.bfloat16, jnp.float32
    blocks = FIELDS + 1
    force[...] = jnp.zeros_like(force)
    record[...] = jnp.zeros_like(record)
    sub = lax.broadcasted_iota(jnp.int32, (16, TILE), 0)
    bit = lax.shift_left(jnp.ones_like(sub), sub & 7)
    upper = sub >= 8
    word_lane = lax.broadcasted_iota(jnp.int32, (16, TILE), 1)
    for f in range(blocks):
        chosen = jnp.where(sub == f, 1.0, 0.0).astype(bf16)
        for part in range(3):
            spread[16 * part : 16 * part + 16, f * TILE : f * TILE + TILE] = chosen
    for k in range(12):
        pick[:, k * TILE : k * TILE + TILE] = jnp.where(sub == k % 6, 1.0, 0.0).astype(bf16)
    ones = jnp.where(sub < 3, 1.0, 0.0).astype(bf16)

    def one_pair(p, t, slot, reach_i, reach_j):
        rad_i = radii[pl.ds(t, 1), :]
        own = [slots[f, pl.ds(t, 1), :] for f in range(FIELDS)]
        own = [-f for f in own[:6]] + [rad_i * w for w in own[6:]] + [rad_i]
        for f in range(blocks):
            rest = jnp.broadcast_to(own[f], (16, TILE))
            high = rest.astype(bf16).astype(f32)
            middle = (rest - high).astype(bf16).astype(f32)
            low = rest - high - middle
            part = jnp.where(sub == 0, high, jnp.where(sub == 1, middle, low))
            spread[48:64, f * TILE : f * TILE + TILE] = part.astype(bf16)
        rad_j_row = radii[pl.ds(slot, 1), :]
        for f in range(FIELDS):
            row = slots[f, pl.ds(slot, 1), :]
            record[f : f + 1, :] = row if f < 6 else rad_j_row * row
        record[FIELDS : FIELDS + 1, :] = rad_j_row
        left = jnp.concatenate(split(record[...], 3) + [ones], axis=0)
        fields[...] = lax.dot_general(
            left, spread[...], (((0,), (0,)), ((), ())), preferred_element_type=f32
        )
        valid = lax.shift_left(jnp.ones_like(sub), jnp.clip(reach_j - 8 * sub, 0, 8)) - 1
        words = jnp.where(word_lane < reach_i, masks[p] & valid, 0)
        radius_i = jnp.broadcast_to(rad_i, (16, TILE))
        sums = [jnp.zeros((16, TILE), f32) for _ in range(6)]
        for c in range(TILE // 16):
            got = [
                fields[16 * c : 16 * c + 16, f * TILE : f * TILE + TILE] for f in range(blocks)
            ]
            sep, change, spin_sum, reach_sum = got[0:3], got[3:6], got[6:9], got[9]
            word = jnp.where(
                upper,
                jnp.broadcast_to(words[2 * c + 1 : 2 * c + 2, :], (16, TILE)),
                jnp.broadcast_to(words[2 * c : 2 * c + 1, :], (16, TILE)),
            )
            on = (word & bit) != 0
            square = (
                sep[0] * sep[0] + sep[1] * sep[1] + (sep[2] * sep[2] + softening * softening)
            )
            inverse = lax.rsqrt(square)
            normal = [s * inverse for s in sep]
            inter = jnp.maximum(reach_sum - square * inverse, 0.0)
            inner = radius_i * (reach_sum - radius_i) * inter
            root = inner * lax.rsqrt(jnp.maximum(inner * reach_sum, 1e-36))
            scale = jnp.where(on, root, 0.0)
            turning = cross(spin_sum, normal)
            slip = [change[k] - turning[k] for k in range(3)]
            speed = slip[0] * normal[0] + slip[1] * normal[1] + slip[2] * normal[2]
            push = scale * (inter - 0.2 * speed)
            drag = 0.3 * scale
            pushed = [push * normal[k] - drag * slip[k] for k in range(3)]
            terms = pushed + list(cross(normal, pushed))
            for k in range(6):
                sums[k] = sums[k] + terms[k]
                high, low = split(terms[k], 2)
                terms_hold[16 * c : 16 * c + 16, k * TILE : k * TILE + TILE] = high
                terms_hold[16 * c : 16 * c + 16, (6 + k) * TILE : (7 + k) * TILE] = low
        others = lax.dot_general(
            pick[...], terms_hold[...], (((1,), (1,)), ((), ())), preferred_element_type=f32
        )
        for k in range(6):
            mine = jnp.sum(sums[k], axis=0, keepdims=True)
            if k >= 3:
                mine = rad_i * mine
            force[k, pl.ds(t, 1), :] = force[k, pl.ds(t, 1), :] - mine
        for k in range(6):
            theirs = others[k : k + 1, :]
            if k >= 3:
                theirs = -rad_j_row * theirs
            force[k, pl.ds(slot, 1), :] = force[k, pl.ds(slot, 1), :] + theirs

    def one(p, carry):
        t = p // PARTNERS
        slot = partner[p]
        reach_i = reach[t]
        reach_j = reach[slot]

        @pl.when(jnp.logical_and(reach_i > 0, reach_j > 0))
        def _():
            one_pair(p, t, slot, reach_i, reach_j)

        return carry

    lax.fori_loop(0, partner.shape[0], one, 0)


def local(sizes, positions, velocities, spins, radii, counts, exports, partners, masks):
    tiles_own = radii.shape[-1] // TILE
    per_side = exports.shape[-1]
    ghosts = 8 * per_side
    slots_all = tiles_own + ghosts
    count = counts[0, 0]
    chosen = exports[0, 0].reshape(-1)
    partner = partners[0, 0]
    words = masks[0, 0]
    starts = TILE * jnp.arange(tiles_own, dtype=jnp.int32)
    own_reach = jnp.clip(count - starts, 0, TILE)
    sent_reach = jnp.clip(count - TILE * exports[0, 0], 0, TILE)
    sent_reach = jnp.pad(sent_reach[:, None, :], ((0, 0), (0, 7), (0, TILE - per_side)))
    index = jnp.arange(tiles_own * TILE, dtype=jnp.int32)
    live = (index < count).astype(jnp.float32).reshape(tiles_own, TILE)
    radius = radii[0, 0].reshape(tiles_own, TILE)
    state = jnp.concatenate([positions[0, 0], velocities[0, 0], spins[0, 0]], axis=0)
    state = state.reshape(FIELDS, tiles_own, TILE)
    places = jnp.arange(tiles_own, dtype=jnp.int32)
    chooser = (places[:, None] == chosen[None, :]).astype(jnp.bfloat16)

    f32 = jnp.float32
    slots_shape = jax.ShapeDtypeStruct((FIELDS, slots_all, TILE), f32)
    state_shape = jax.ShapeDtypeStruct((FIELDS, tiles_own, TILE), f32)
    sent = pltpu.VMEM((FIELDS, ghosts, TILE), f32)
    back = pltpu.VMEM((6, ghosts, TILE), f32)
    dma = pltpu.SemaphoreType.DMA((8,))

    def params(number):
        return pltpu.CompilerParams(
            collective_id=number, has_side_effects=True, vmem_limit_bytes=LIMIT
        )

    slots, radii_all, reaches = pl.pallas_call(
        functools.partial(first_kernel, sizes, per_side, tiles_own),
        out_shape=(
            slots_shape,
            jax.ShapeDtypeStruct((slots_all, TILE), f32),
            jax.ShapeDtypeStruct((8, 8, TILE), jnp.int32),
        ),
        in_specs=[SMEM, VMEM, VMEM, VMEM],
        out_specs=(VMEM, VMEM, VMEM),
        scratch_shapes=[sent, pltpu.VMEM((ghosts, TILE), f32)] + [dma] * 6,
        compiler_params=params(0),
        name="send_first",
    )(chosen, state, radius, sent_reach)
    reach = jnp.concatenate([own_reach, reaches[:, 0, :per_side].reshape(-1)])

    def pair_forces(slots):
        return pl.pallas_call(
            functools.partial(pair_kernel, tiles_own),
            out_shape=jax.ShapeDtypeStruct((6, slots_all, TILE), f32),
            in_specs=[SMEM, SMEM, VMEM, VMEM, VMEM],
            out_specs=VMEM,
            scratch_shapes=[
                pltpu.VMEM((16, TILE), f32),
                pltpu.VMEM((64, (FIELDS + 1) * TILE), jnp.bfloat16),
                pltpu.VMEM((TILE, (FIELDS + 1) * TILE), f32),
                pltpu.VMEM((TILE, 12 * TILE), jnp.bfloat16),
                pltpu.VMEM((16, 12 * TILE), jnp.bfloat16),
            ],
            compiler_params=pltpu.CompilerParams(vmem_limit_bytes=LIMIT),
            name="pair_forces",
        )(partner, reach, slots, radii_all, words)

    for step in range(STEPS):
        force = pair_forces(slots)
        if step < STEPS - 1:
            state, slots = pl.pallas_call(
                functools.partial(middle_kernel, sizes, per_side, tiles_own),
                out_shape=(state_shape, slots_shape),
                in_specs=[SMEM] + [VMEM] * 5,
                out_specs=(VMEM, VMEM),
                scratch_shapes=[sent, back] + [dma] * 4,
                compiler_params=params(1 + step),
                name="return_advance_send",
            )(chosen, chooser, state, radius, live, force)
        else:
            state = pl.pallas_call(
                functools.partial(last_kernel, sizes, per_side, tiles_own),
                out_shape=state_shape,
                in_specs=[VMEM] * 5,
                out_specs=VMEM,
                scratch_shapes=[back] + [dma] * 2,
                compiler_params=params(1 + step),
                name="return_advance",
            )(chooser, state, radius, live, force)
    shape = (1, 1, 3, tiles_own * TILE)
    return tuple(state[3 * k : 3 * k + 3].reshape(shape) for k in range(3))


def solution(mesh):
    sizes = (mesh.shape["gx"], mesh.shape["gy"])
    return jax.shard_map(
        functools.partial(local, sizes),
        mesh=mesh,
        in_specs=(
            P("gx", "gy", None, None),
            P("gx", "gy", None, None),
            P("gx", "gy", None, None),
            P("gx", "gy", None),
            P("gx", "gy"),
            P("gx", "gy", None, None),
            P("gx", "gy", None),
            P("gx", "gy", None, None, None),
        ),
        out_specs=(P("gx", "gy", None, None), P("gx", "gy", None, None), P("gx", "gy", None, None)),
        check_vma=False,
    )
```

```python
import functools

import jax
import jax.numpy as jnp
from jax import lax
from jax.experimental import pallas as pl
from jax.experimental.pallas import tpu as pltpu
from jax.sharding import PartitionSpec as P

TILE = 128
PARTNERS = 2
STEPS = 2
FIELDS = 9

softening = 0.05
time_step = 0.25
column_width = 3.0
gravity = 1.0
mass_scale = 8.0
offsets = ((1, 0), (-1, 0), (0, 1), (0, -1), (1, 1), (1, -1), (-1, 1), (-1, -1))
order = (2, 3, 4, 5, 6, 7, 0, 1)

MESH = pl.DeviceIdType.MESH
VMEM = pl.BlockSpec(memory_space=pltpu.VMEM)
SMEM = pl.BlockSpec(memory_space=pltpu.SMEM)
LIMIT = 40 * 1024 * 1024


def neighbour(sizes, which, sign):
    a, b = offsets[which]
    nx, ny = sizes
    x = lax.rem(lax.axis_index("gx") + sign * a + nx, nx)
    y = lax.rem(lax.axis_index("gy") + sign * b + ny, ny)
    return (x, y)


def greet(sizes):
    barrier = pltpu.get_barrier_semaphore()
    for which in range(8):
        pl.semaphore_signal(
            barrier, inc=1, device_id=neighbour(sizes, which, 1), device_id_type=MESH
        )
    pl.semaphore_wait(barrier, 8)


def gather_tiles(chosen, state, sent, which, per_side):
    a, b = offsets[which]
    moved = (-a * column_width, -b * column_width)

    def one(e, carry):
        tile = chosen[which * per_side + e]
        for f in range(FIELDS):
            row = state[f, pl.ds(tile, 1), :]
            if f < 2 and moved[f] != 0.0:
                row = row + moved[f]
            sent[f, pl.ds(which * per_side + e, 1), :] = row
        return carry

    lax.fori_loop(0, per_side, one, 0, unroll=4)


def send_records(sizes, chosen, state, sent, slots, send_sem, recv_sem, per_side, tiles_own):
    copies = []
    for which in order:
        gather_tiles(chosen, state, sent, which, per_side)
        copy = pltpu.make_async_remote_copy(
            src_ref=sent.at[:, pl.ds(which * per_side, per_side), :],
            dst_ref=slots.at[:, pl.ds(tiles_own + which * per_side, per_side), :],
            send_sem=send_sem.at[which],
            recv_sem=recv_sem.at[which],
            device_id=neighbour(sizes, which, 1),
            device_id_type=MESH,
        )
        copy.start()
        copies.append(copy)
    slots[:, 0:tiles_own, :] = state[...]
    return copies


def first_kernel(
    sizes, per_side, tiles_own, chosen, state, radius, reach,
    slots, radii, reaches, sent, sent_radius, send_sem, recv_sem, rad_send, rad_recv,
    reach_send, reach_recv,
):
    greet(sizes)
    copies = send_records(
        sizes, chosen, state, sent, slots, send_sem, recv_sem, per_side, tiles_own
    )
    for which in order:
        def one(e, carry):
            tile = chosen[which * per_side + e]
            sent_radius[pl.ds(which * per_side + e, 1), :] = radius[pl.ds(tile, 1), :]
            return carry

        lax.fori_loop(0, per_side, one, 0, unroll=4)
        to = neighbour(sizes, which, 1)
        copy = pltpu.make_async_remote_copy(
            src_ref=sent_radius.at[pl.ds(which * per_side, per_side), :],
            dst_ref=radii.at[pl.ds(tiles_own + which * per_side, per_side), :],
            send_sem=rad_send.at[which],
            recv_sem=rad_recv.at[which],
            device_id=to,
            device_id_type=MESH,
        )
        copy.start()
        copies.append(copy)
        copy = pltpu.make_async_remote_copy(
            src_ref=reach.at[which],
            dst_ref=reaches.at[which],
            send_sem=reach_send.at[which],
            recv_sem=reach_recv.at[which],
            device_id=to,
            device_id_type=MESH,
        )
        copy.start()
        copies.append(copy)
    radii[0:tiles_own, :] = radius[...]
    for copy in copies:
        copy.wait()


def start_returns(sizes, force, back, send_sem, recv_sem, per_side, tiles_own):
    copies = []
    for which in order:
        copy = pltpu.make_async_remote_copy(
            src_ref=force.at[:, pl.ds(tiles_own + which * per_side, per_side), :],
            dst_ref=back.at[:, pl.ds(which * per_side, per_side), :],
            send_sem=send_sem.at[which],
            recv_sem=recv_sem.at[which],
            device_id=neighbour(sizes, which, -1),
            device_id_type=MESH,
        )
        copy.start()
        copies.append(copy)
    return copies


def advance(chooser, state, radius, live, force, back, moved, tiles_own):
    rad = radius[...]
    alive = time_step * live[...]
    mass = mass_scale * rad * rad * rad
    inertia = 0.4 * mass * rad * rad
    hot = chooser[...]
    total = []
    for f in range(6):
        values = back[f]
        high = values.astype(jnp.bfloat16)
        rest = values - high.astype(jnp.float32)
        middle = rest.astype(jnp.bfloat16)
        low = (rest - middle.astype(jnp.float32)).astype(jnp.bfloat16)
        summed = force[f, 0:tiles_own, :]
        for part in (low, middle, high):
            summed = summed + jnp.dot(hot, part, preferred_element_type=jnp.float32)
        total.append(summed)
    for k in range(3):
        pull = total[k] / mass
        if k == 2:
            pull = pull - gravity
        velocity = state[3 + k] + alive * pull
        moved[3 + k] = velocity
        moved[6 + k] = state[6 + k] + alive * total[3 + k] / inertia
        moved[k] = state[k] + alive * velocity


def middle_kernel(
    sizes, per_side, tiles_own, chosen, chooser, state, radius, live, force,
    moved, slots, sent, back, back_send, back_recv, send_sem, recv_sem,
):
    greet(sizes)
    for copy in start_returns(sizes, force, back, back_send, back_recv, per_side, tiles_own):
        copy.wait()
    advance(chooser, state, radius, live, force, back, moved, tiles_own)
    copies = send_records(
        sizes, chosen, moved, sent, slots, send_sem, recv_sem, per_side, tiles_own
    )
    for copy in copies:
        copy.wait()


def last_kernel(
    sizes, per_side, tiles_own, chooser, state, radius, live, force,
    moved, back, back_send, back_recv,
):
    greet(sizes)
    for copy in start_returns(sizes, force, back, back_send, back_recv, per_side, tiles_own):
        copy.wait()
    advance(chooser, state, radius, live, force, back, moved, tiles_own)


def cross(left, right):
    return (
        left[1] * right[2] - left[2] * right[1],
        left[2] * right[0] - left[0] * right[2],
        left[0] * right[1] - left[1] * right[0],
    )


def split(values, parts):
    pieces = []
    for _ in range(parts - 1):
        piece = values.astype(jnp.bfloat16)
        pieces.append(piece)
        values = values - piece.astype(jnp.float32)
    return pieces + [values.astype(jnp.bfloat16)]


def pair_kernel(
    tiles_own, partner, reach, slots, radii, masks, force,
    record_0, record_1, spread_0, spread_1, fields_0, fields_1, terms_0, terms_1, pick, listed,
):
    bf16, f32 = jnp.bfloat16, jnp.float32
    blocks = FIELDS + 1
    force[...] = jnp.zeros_like(force)
    record_0[...] = jnp.zeros_like(record_0)
    record_1[...] = jnp.zeros_like(record_1)
    terms_1[...] = jnp.zeros_like(terms_1)
    sub = lax.broadcasted_iota(jnp.int32, (16, TILE), 0)
    bit = lax.shift_left(jnp.ones_like(sub), sub & 7)
    upper = sub >= 8
    word_lane = lax.broadcasted_iota(jnp.int32, (16, TILE), 1)
    for f in range(blocks):
        chosen = jnp.where(sub == f, 1.0, 0.0).astype(bf16)
        for part in range(3):
            for spread in (spread_0, spread_1):
                spread[16 * part : 16 * part + 16, f * TILE : f * TILE + TILE] = chosen
    for k in range(12):
        pick[:, k * TILE : k * TILE + TILE] = jnp.where(sub == k % 6, 1.0, 0.0).astype(bf16)
    ones = jnp.where(sub < 3, 1.0, 0.0).astype(bf16)

    def note_live(p, number):
        listed[number] = p
        both = jnp.logical_and(reach[p // PARTNERS] > 0, reach[partner[p]] > 0)
        return number + jnp.where(both, 1, 0)

    number = lax.fori_loop(0, partner.shape[0], note_live, 0, unroll=4)

    def find(at):
        p = listed[jnp.clip(at, 0, jnp.maximum(number - 1, 0))]
        t = p // PARTNERS
        slot = partner[p]
        return p, t, slot, jnp.where(at < number, reach[t], 0), reach[slot]

    def prepare(pair, record, spread, fields):
        p, t, slot, reach_i, reach_j = pair
        rad_i = radii[pl.ds(t, 1), :]
        own = [slots[f, pl.ds(t, 1), :] for f in range(FIELDS)]
        own = [-f for f in own[:6]] + [rad_i * w for w in own[6:]] + [rad_i]
        for f in range(blocks):
            rest = jnp.broadcast_to(own[f], (16, TILE))
            high = rest.astype(bf16).astype(f32)
            middle = (rest - high).astype(bf16).astype(f32)
            low = rest - high - middle
            part = jnp.where(sub == 0, high, jnp.where(sub == 1, middle, low))
            spread[48:64, f * TILE : f * TILE + TILE] = part.astype(bf16)
        rad_j_row = radii[pl.ds(slot, 1), :]
        for f in range(FIELDS):
            row = slots[f, pl.ds(slot, 1), :]
            record[f : f + 1, :] = row if f < 6 else rad_j_row * row
        record[FIELDS : FIELDS + 1, :] = rad_j_row
        left = jnp.concatenate(split(record[...], 3) + [ones], axis=0)
        fields[...] = lax.dot_general(
            left, spread[...], (((0,), (0,)), ((), ())), preferred_element_type=f32
        )

    def compute(pair, fields, terms_hold):
        p, t, slot, reach_i, reach_j = pair
        rad_i = radii[pl.ds(t, 1), :]
        valid = lax.shift_left(jnp.ones_like(sub), jnp.clip(reach_j - 8 * sub, 0, 8)) - 1
        words = jnp.where(word_lane < reach_i, masks[p] & valid, 0)
        radius_i = jnp.broadcast_to(rad_i, (16, TILE))
        sums = [jnp.zeros((16, TILE), f32) for _ in range(6)]
        for c in range(TILE // 16):
            got = [
                fields[16 * c : 16 * c + 16, f * TILE : f * TILE + TILE] for f in range(blocks)
            ]
            sep, change, spin_sum, reach_sum = got[0:3], got[3:6], got[6:9], got[9]
            word = jnp.where(
                upper,
                jnp.broadcast_to(words[2 * c + 1 : 2 * c + 2, :], (16, TILE)),
                jnp.broadcast_to(words[2 * c : 2 * c + 1, :], (16, TILE)),
            )
            on = (word & bit) != 0
            square = (
                sep[0] * sep[0] + sep[1] * sep[1] + (sep[2] * sep[2] + softening * softening)
            )
            inverse = lax.rsqrt(square)
            normal = [s * inverse for s in sep]
            inter = jnp.maximum(reach_sum - square * inverse, 0.0)
            inner = radius_i * (reach_sum - radius_i) * inter
            root = inner * lax.rsqrt(jnp.maximum(inner * reach_sum, 1e-36))
            scale = jnp.where(on, root, 0.0)
            turning = cross(spin_sum, normal)
            slip = [change[k] - turning[k] for k in range(3)]
            speed = slip[0] * normal[0] + slip[1] * normal[1] + slip[2] * normal[2]
            push = scale * (inter - 0.2 * speed)
            drag = 0.3 * scale
            pushed = [push * normal[k] - drag * slip[k] for k in range(3)]
            terms = pushed + list(cross(normal, pushed))
            for k in range(6):
                sums[k] = sums[k] + terms[k]
                high, low = split(terms[k], 2)
                terms_hold[16 * c : 16 * c + 16, k * TILE : k * TILE + TILE] = high
                terms_hold[16 * c : 16 * c + 16, (6 + k) * TILE : (7 + k) * TILE] = low
        for k in range(6):
            mine = jnp.sum(sums[k], axis=0, keepdims=True)
            if k >= 3:
                mine = rad_i * mine
            force[k, pl.ds(t, 1), :] = force[k, pl.ds(t, 1), :] - mine

    def reduce(pair, terms_hold):
        slot = pair[2]
        others = lax.dot_general(
            pick[...], terms_hold[...], (((1,), (1,)), ((), ())), preferred_element_type=f32
        )
        rad_j_row = radii[pl.ds(slot, 1), :]
        for k in range(6):
            theirs = others[k : k + 1, :]
            if k >= 3:
                theirs = -rad_j_row * theirs
            force[k, pl.ds(slot, 1), :] = force[k, pl.ds(slot, 1), :] + theirs

    prepare(find(0), record_0, spread_0, fields_0)
    rounds = (number + 1) // 2

    def two_pairs(m, carry):
        before, first, second, later = (find(2 * m + k) for k in (-1, 0, 1, 2))
        prepare(second, record_1, spread_1, fields_1)
        reduce(before, terms_1)
        compute(first, fields_0, terms_0)
        prepare(later, record_0, spread_0, fields_0)
        reduce(first, terms_0)
        compute(second, fields_1, terms_1)
        return carry

    lax.fori_loop(0, rounds, two_pairs, 0)
    reduce(find(2 * rounds - 1), terms_1)


def local(sizes, positions, velocities, spins, radii, counts, exports, partners, masks):
    tiles_own = radii.shape[-1] // TILE
    per_side = exports.shape[-1]
    ghosts = 8 * per_side
    slots_all = tiles_own + ghosts
    count = counts[0, 0]
    chosen = exports[0, 0].reshape(-1)
    partner = partners[0, 0]
    words = masks[0, 0]
    starts = TILE * jnp.arange(tiles_own, dtype=jnp.int32)
    own_reach = jnp.clip(count - starts, 0, TILE)
    sent_reach = jnp.clip(count - TILE * exports[0, 0], 0, TILE)
    sent_reach = jnp.pad(sent_reach[:, None, :], ((0, 0), (0, 7), (0, TILE - per_side)))
    index = jnp.arange(tiles_own * TILE, dtype=jnp.int32)
    live = (index < count).astype(jnp.float32).reshape(tiles_own, TILE)
    radius = radii[0, 0].reshape(tiles_own, TILE)
    state = jnp.concatenate([positions[0, 0], velocities[0, 0], spins[0, 0]], axis=0)
    state = state.reshape(FIELDS, tiles_own, TILE)
    places = jnp.arange(tiles_own, dtype=jnp.int32)
    chooser = (places[:, None] == chosen[None, :]).astype(jnp.bfloat16)

    f32 = jnp.float32
    slots_shape = jax.ShapeDtypeStruct((FIELDS, slots_all, TILE), f32)
    state_shape = jax.ShapeDtypeStruct((FIELDS, tiles_own, TILE), f32)
    sent = pltpu.VMEM((FIELDS, ghosts, TILE), f32)
    back = pltpu.VMEM((6, ghosts, TILE), f32)
    dma = pltpu.SemaphoreType.DMA((8,))

    def params(number):
        return pltpu.CompilerParams(
            collective_id=number, has_side_effects=True, vmem_limit_bytes=LIMIT
        )

    slots, radii_all, reaches = pl.pallas_call(
        functools.partial(first_kernel, sizes, per_side, tiles_own),
        out_shape=(
            slots_shape,
            jax.ShapeDtypeStruct((slots_all, TILE), f32),
            jax.ShapeDtypeStruct((8, 8, TILE), jnp.int32),
        ),
        in_specs=[SMEM, VMEM, VMEM, VMEM],
        out_specs=(VMEM, VMEM, VMEM),
        scratch_shapes=[sent, pltpu.VMEM((ghosts, TILE), f32)] + [dma] * 6,
        compiler_params=params(0),
        name="send_first",
    )(chosen, state, radius, sent_reach)
    reach = jnp.concatenate([own_reach, reaches[:, 0, :per_side].reshape(-1)])

    def pair_forces(slots):
        return pl.pallas_call(
            functools.partial(pair_kernel, tiles_own),
            out_shape=jax.ShapeDtypeStruct((6, slots_all, TILE), f32),
            in_specs=[SMEM, SMEM, VMEM, VMEM, VMEM],
            out_specs=VMEM,
            scratch_shapes=[
                *[pltpu.VMEM((16, TILE), f32)] * 2,
                *[pltpu.VMEM((64, (FIELDS + 1) * TILE), jnp.bfloat16)] * 2,
                *[pltpu.VMEM((TILE, (FIELDS + 1) * TILE), f32)] * 2,
                *[pltpu.VMEM((TILE, 12 * TILE), jnp.bfloat16)] * 2,
                pltpu.VMEM((16, 12 * TILE), jnp.bfloat16),
                pltpu.SMEM((partner.shape[0] + 1,), jnp.int32),
            ],
            compiler_params=pltpu.CompilerParams(vmem_limit_bytes=LIMIT),
            name="pair_forces",
        )(partner, reach, slots, radii_all, words)

    for step in range(STEPS):
        force = pair_forces(slots)
        if step < STEPS - 1:
            state, slots = pl.pallas_call(
                functools.partial(middle_kernel, sizes, per_side, tiles_own),
                out_shape=(state_shape, slots_shape),
                in_specs=[SMEM] + [VMEM] * 5,
                out_specs=(VMEM, VMEM),
                scratch_shapes=[sent, back] + [dma] * 4,
                compiler_params=params(1 + step),
                name="return_advance_send",
            )(chosen, chooser, state, radius, live, force)
        else:
            state = pl.pallas_call(
                functools.partial(last_kernel, sizes, per_side, tiles_own),
                out_shape=state_shape,
                in_specs=[VMEM] * 5,
                out_specs=VMEM,
                scratch_shapes=[back] + [dma] * 2,
                compiler_params=params(1 + step),
                name="return_advance",
            )(chooser, state, radius, live, force)
    shape = (1, 1, 3, tiles_own * TILE)
    return tuple(state[3 * k : 3 * k + 3].reshape(shape) for k in range(3))


def solution(mesh):
    sizes = (mesh.shape["gx"], mesh.shape["gy"])
    return jax.shard_map(
        functools.partial(local, sizes),
        mesh=mesh,
        in_specs=(
            P("gx", "gy", None, None),
            P("gx", "gy", None, None),
            P("gx", "gy", None, None),
            P("gx", "gy", None),
            P("gx", "gy"),
            P("gx", "gy", None, None),
            P("gx", "gy", None),
            P("gx", "gy", None, None, None),
        ),
        out_specs=(P("gx", "gy", None, None), P("gx", "gy", None, None), P("gx", "gy", None, None)),
        check_vma=False,
    )
```
